32 devices in a mesh: grp: 4 (over y, x), row: 8 (over z, core).
Axes of the slice: x: 2, y: 2, z: 4, core: 2. Of those that a mesh axis runs over, the one named last changes fastest.
Arguments:
- snapshots: float32 [16, 4, 65536], P('grp', None, 'row'), may hold values from -12 to 12
- basis: float32 [128, 262144], P(None, ('grp', 'row')), may hold values from -4 to 4
- assignment: int32 [16], replicated, may hold values from 0 to 15, each once
- param_index: int32 [16], replicated, may hold values from 0 to 63
- offsets: int32 [8, 262144], P(None, ('grp', 'row')), may hold values from -2048 to 2048, as said below
- coefs: float32 [2, 8, 262144], P(None, None, ('grp', 'row')), may hold values from -2.5 to 2.5
Outputs:
- new_columns: float32 [16, 262144], P(None, ('grp', 'row'))
- applied: float32 [2, 16, 262144], P(None, None, ('grp', 'row'))
- coords: float32 [128, 16], replicated
- r_factor: float32 [16, 16], replicated
- reduced: float32 [2, 144, 16], replicated
- estimate: float32 [16], replicated
The draws below stay inside these ranges and needn't reach their ends.
Inputs may be any that keep to these rules, and one draw needn't show every extreme that they name: `offsets`: both ends of the range occur in every draw.
All inputs are finite; a program needn't handle non-finite values.
Results may differ from the reference program's by a relative error of at most 0.00029.
Values sent between devices are 32-bit elements; how exact they have to be, the bound alone decides.
A program may use at most 64 MiB of HBM per device.

```python
import jax
import jax.numpy as jnp
from jax import lax

NB = 128
NSNAP = 16
KTERMS = 2
NNZ = 8
NPARAM = 64
HALO = 2048
ROWS = 262144
N_GRP = 4


def make_basis(key):
    inner = jax.random.fold_in(key, 11)
    values = jax.random.normal(inner, (NB, ROWS), jnp.float32)
    column_order = jax.random.permutation(jax.random.fold_in(key, 12), NB)
    first_mix = jax.random.uniform(jax.random.fold_in(key, 13), (NB, 1), jnp.float32, 0.3, 0.6)
    second_mix = jax.random.uniform(jax.random.fold_in(key, 14), (NB, 1), jnp.float32, -0.2, 0.2)
    lined = values[column_order]
    prev_one = jnp.concatenate([jnp.zeros((1, ROWS), jnp.float32), lined[:-1]], axis=0)
    prev_two = jnp.concatenate([jnp.zeros((2, ROWS), jnp.float32), lined[:-2]], axis=0)
    mixed = lined + first_mix * prev_one + second_mix * prev_two
    back_order = jnp.argsort(column_order)
    values = mixed[back_order]
    return jnp.clip(values, -4.0, 4.0)


def draw_basis(key, part):
    return make_basis(key)


def draw_snapshots(key, part):
    basis = make_basis(key)
    weights = 0.3 * jax.random.normal(jax.random.fold_in(key, 21), (NSNAP, NB), jnp.float32)
    spread = jnp.arange(ROWS, dtype=jnp.float32) / ROWS
    trend = 3.0 ** (0.5 * spread)
    rough = jnp.exp(jax.random.uniform(jax.random.fold_in(key, 22), (NSNAP, ROWS), jnp.float32, 0.0, 1.1))
    fresh = 0.5 * jax.random.normal(jax.random.fold_in(key, 23), (NSNAP, ROWS), jnp.float32)
    column_scale = jnp.exp(jax.random.uniform(jax.random.fold_in(key, 24), (NSNAP, 1), jnp.float32, -0.7, 0.7))
    values = jnp.dot(weights, basis) + fresh * rough * trend[None, :] * column_scale
    values = jnp.clip(values, -12.0, 12.0)
    return values.reshape(NSNAP, N_GRP, ROWS // N_GRP)


def draw_offsets(key, part):
    values = jax.random.randint(jax.random.fold_in(key, 31), (NNZ, ROWS), -HALO, HALO + 1, jnp.int32)
    values = values.at[0, 0].set(-HALO)
    values = values.at[NNZ - 1, ROWS - 1].set(HALO)
    return values


def set_ends(drawn, own_key, least, high):
    longest = drawn.shape.index(max(drawn.shape))
    spots = []
    for shift in (0, 1):
        where = [jax.random.randint(jax.random.fold_in(own_key, axis), (), 0, length) for axis, length in enumerate(drawn.shape)]
        where[longest] = (where[longest] + shift) % drawn.shape[longest]
        spots.append(tuple(where))
    return drawn.at[spots[0]].set(least).at[spots[1]].set(high)


def levels(key, dims, shards, least, high):
    level = 1.0
    for axis_at, blocks in shards:
        steps = jax.random.uniform(jax.random.fold_in(jax.random.fold_in(key, 6), axis_at), (blocks,), jnp.float32, least / len(shards), high / len(shards))
        level = level * jnp.repeat(jnp.exp(steps), dims[axis_at] // blocks).reshape((-1,) + (1,) * (len(dims) - 1 - axis_at))
    return level


def scatter_about(rng, dims, scale, most, pieces=(), held_as=jnp.bfloat16):
    array = jax.random.normal(rng, dims, jnp.float32) * scale
    if len(pieces) > 0:
        array = levels(rng, dims, pieces, -0.22, 0.18) * array
    return jnp.clip(array, min=-most, max=most).astype(held_as)


def setup_inputs(seed: int = 0) -> dict:
    arg_keys = jax.random.split(jax.random.key(seed), 7)
    return {
        "snapshots": draw_snapshots(jax.random.fold_in(arg_keys[6], 71), 0),
        "basis": draw_basis(jax.random.fold_in(arg_keys[6], 71), 0),
        "assignment": jax.random.permutation(arg_keys[2], NSNAP).astype(jnp.int32),
        "param_index": set_ends(jax.random.randint(arg_keys[3], (NSNAP,), 0, NPARAM), jax.random.fold_in(arg_keys[3], 1), 0, NPARAM - 1).astype(jnp.int32),
        "offsets": draw_offsets(jax.random.fold_in(arg_keys[6], 71), 0),
        "coefs": scatter_about(arg_keys[5], (KTERMS, NNZ, ROWS), 0.35, 2.5, ((2, 32),), jnp.float32),
    }


def cholesky_lower(matrix):
    order = matrix.shape[0]
    index_list = jnp.arange(order, dtype=jnp.int32)

    def step(column_index, factor):
        column = lax.dynamic_slice_in_dim(matrix, column_index, 1, 1)[:, 0]
        factor_row = lax.dynamic_slice_in_dim(factor, column_index, 1, 0)[0]
        column = column - jnp.dot(factor, factor_row, precision=lax.Precision.HIGHEST)
        pivot = jnp.sqrt(jnp.sum(jnp.where(index_list == column_index, column, 0.0)))
        fresh = jnp.where(index_list > column_index, column / pivot, jnp.where(index_list == column_index, pivot, 0.0))
        return lax.dynamic_update_slice_in_dim(factor, fresh[:, None], column_index, 1)
    return lax.fori_loop(0, order, step, jnp.zeros(matrix.shape, matrix.dtype))

def forward_solve(lower, right):
    order = lower.shape[0]

    def step(row_index, solved):
        lower_row = lax.dynamic_slice_in_dim(lower, row_index, 1, 0)[0]
        pivot = jnp.sum(jnp.where(jnp.arange(order, dtype=jnp.int32) == row_index, lower_row, 0.0))
        target = lax.dynamic_slice_in_dim(right, row_index, 1, 0)[0]
        value = (target - jnp.dot(lower_row, solved, precision=lax.Precision.HIGHEST)) / pivot
        return lax.dynamic_update_slice_in_dim(solved, value[None, :], row_index, 0)
    return lax.fori_loop(0, order, step, jnp.zeros(right.shape, right.dtype))

def backward_solve(lower, right):
    order = lower.shape[0]

    def step(turn, solved):
        row_index = order - 1 - turn
        upper_row = lax.dynamic_slice_in_dim(lower, row_index, 1, 1)[:, 0]
        pivot = jnp.sum(jnp.where(jnp.arange(order, dtype=jnp.int32) == row_index, upper_row, 0.0))
        target = lax.dynamic_slice_in_dim(right, row_index, 1, 0)[0]
        value = (target - jnp.dot(upper_row, solved, precision=lax.Precision.HIGHEST)) / pivot
        return lax.dynamic_update_slice_in_dim(solved, value[None, :], row_index, 0)
    return lax.fori_loop(0, order, step, jnp.zeros(right.shape, right.dtype))

def apply_sparse(fields, offsets, coefs, width):
    row_count = fields.shape[1]
    extended = jnp.pad(fields, ((0, 0), (width, width)))
    positions = jnp.arange(row_count, dtype=jnp.int32) + width
    totals = [jnp.zeros(fields.shape, fields.dtype) for term_index in range(coefs.shape[0])]
    for slot_index in range(offsets.shape[0]):
        picked = jnp.take(extended, (positions + offsets[slot_index]).astype(jnp.int32), axis=1)
        totals = [totals[term_index] + coefs[term_index, slot_index][None, :] * picked for term_index in range(len(totals))]
    return jnp.stack(totals)

def reference(snapshots, basis, assignment, param_index, offsets, coefs):
    highest = lax.Precision.HIGHEST
    arrived = snapshots.reshape(NSNAP, ROWS)
    placing = (assignment[None, :] == jnp.arange(NSNAP, dtype=jnp.int32)[:, None]).astype(arrived.dtype)
    ordered = jnp.dot(placing, arrived, precision=highest)
    gram = jnp.dot(basis, basis.T, precision=highest) / ROWS
    project = jnp.dot(basis, ordered.T, precision=highest) / ROWS
    basis_lower = cholesky_lower(gram)
    halfway = forward_solve(basis_lower, project)
    coords = backward_solve(basis_lower, halfway)
    residual = ordered - jnp.dot(coords.T, basis, precision=highest)
    residual_gram = jnp.dot(residual, residual.T, precision=highest) / ROWS
    lower = cholesky_lower(residual_gram)
    inverse = forward_solve(lower, jnp.eye(NSNAP, dtype=residual.dtype))
    new_columns = jnp.dot(inverse, residual, precision=highest)
    applied = apply_sparse(new_columns, offsets, coefs, HALO)
    blocks = []
    for term_index in range(KTERMS):
        upper_part = jnp.dot(basis, applied[term_index].T, precision=highest)
        lower_part = jnp.dot(new_columns, applied[term_index].T, precision=highest)
        blocks.append(jnp.concatenate([upper_part, lower_part], axis=0))
    reduced = jnp.stack(blocks) / ROWS
    viscosity = 0.5 + param_index.astype(arrived.dtype) / NPARAM
    combined = applied[0]
    for term_index in range(1, KTERMS):
        combined = combined + (viscosity ** term_index)[:, None] * applied[term_index]
    estimate = lax.optimization_barrier(jnp.sum(combined * combined, axis=1)) / ROWS
    return (new_columns, applied, coords, lower.T, reduced, estimate)
```

```python
import functools

import jax
import jax.numpy as jnp
from jax import lax
from jax.experimental import pallas as pl
from jax.experimental.pallas import tpu as pltpu
from jax.sharding import PartitionSpec as P

NPARAM = 64
HALO_BLOCKS = 16
F32 = jnp.float32
BF16 = jnp.bfloat16
MESH = pl.DeviceIdType.MESH
NT = (((1,), (1,)), ((), ()))
NN = (((1,), (0,)), ((), ()))


def split(x):
    high = x.astype(BF16)
    low = (x - high.astype(F32)).astype(BF16)
    return high, low


def bdot(a, b, dims):
    return lax.dot_general(a, b, dims, preferred_element_type=F32)


def hdot(a, b, dims=NN):
    return lax.dot_general(a, b, dims, precision=lax.Precision.HIGHEST, preferred_element_type=F32)


def gram_kernel(basis_ref, arrived_ref, out_ref, bb, ab, aa):
    step = pl.program_id(0)

    @pl.when(step == 0)
    def _():
        bb[...] = jnp.zeros_like(bb)
        ab[...] = jnp.zeros_like(ab)
        aa[...] = jnp.zeros_like(aa)

    x = jnp.concatenate(split(basis_ref[...]), axis=0)
    y = jnp.concatenate(split(arrived_ref[...]), axis=0)
    bb[...] += bdot(x, x, NT)
    ab[...] += bdot(y, x, NT)
    aa[...] += bdot(y, y, NT)

    @pl.when(step == pl.num_programs(0) - 1)
    def _():
        nb, ns = basis_ref.shape[0], arrived_ref.shape[0]
        g = bb[...]
        out_ref[0:nb, :] = (g[:nb, :nb] + g[nb:, nb:]) + (g[:nb, nb:] + g[nb:, :nb])
        c = ab[...]
        out_ref[nb : nb + ns, :] = (c[:ns, :nb] + c[ns:, nb:]) + (c[:ns, nb:] + c[ns:, :nb])
        s = aa[...]
        out_ref[nb + ns :, :] = jnp.zeros((ns, nb), F32)
        out_ref[nb + ns :, 0:ns] = (s[:ns, :ns] + s[ns:, ns:]) + (s[:ns, ns:] + s[ns:, :ns])


def gram_sums(basis, arrived, chunk):
    nb, rows = basis.shape
    ns = arrived.shape[0]
    return pl.pallas_call(
        gram_kernel,
        grid=(rows // chunk,),
        in_specs=[
            pl.BlockSpec((nb, chunk), lambda i: (0, i)),
            pl.BlockSpec((ns, chunk), lambda i: (0, i)),
        ],
        out_specs=pl.BlockSpec((nb + 2 * ns, nb), lambda i: (0, 0)),
        out_shape=jax.ShapeDtypeStruct((nb + 2 * ns, nb), F32),
        scratch_shapes=[
            pltpu.VMEM((2 * nb, 2 * nb), F32),
            pltpu.VMEM((2 * ns, 2 * nb), F32),
            pltpu.VMEM((2 * ns, 2 * ns), F32),
        ],
        compiler_params=pltpu.CompilerParams(vmem_limit_bytes=32 << 20),
        name="gram_sums",
    )(basis, arrived)


def reduce_kernel(n_row, count, x_ref, out_ref, held, send1, recv1, send2, recv2):
    tiles = x_ref.shape[0]
    stride = count // tiles
    me = lax.axis_index("grp") * n_row + lax.axis_index("row")
    mine = me // stride
    owner = jnp.logical_and(me == mine * stride, mine < tiles)

    def where(device):
        return (device // n_row, lax.rem(device, n_row))

    barrier = pltpu.get_barrier_semaphore()

    def greet(k, carry):
        pl.semaphore_signal(
            barrier, inc=1, device_id=where(lax.rem(me + k, count)), device_id_type=MESH
        )
        return carry

    lax.fori_loop(1, count, greet, 0)
    pl.semaphore_wait(barrier, count - 1)

    def first(tile):
        return pltpu.make_async_remote_copy(
            src_ref=x_ref.at[tile],
            dst_ref=held.at[me],
            send_sem=send1.at[tile],
            recv_sem=recv1.at[me],
            device_id=where(tile * stride),
            device_id_type=MESH,
        )

    def send_first(k, carry):
        tile = lax.rem(mine + k, tiles)

        @pl.when(tile * stride != me)
        def _():
            first(tile).start()

        return carry

    lax.fori_loop(0, tiles, send_first, 0)

    def second(device):
        return pltpu.make_async_remote_copy(
            src_ref=out_ref.at[mine],
            dst_ref=out_ref.at[mine],
            send_sem=send2.at[device],
            recv_sem=recv2.at[mine],
            device_id=where(device),
            device_id_type=MESH,
        )

    @pl.when(owner)
    def _():
        held[me] = x_ref[mine]

        def landed(k, carry):
            source = lax.rem(me + k, count)
            pltpu.make_async_remote_copy(
                src_ref=x_ref.at[mine],
                dst_ref=held.at[source],
                send_sem=send1.at[mine],
                recv_sem=recv1.at[source],
                device_id=where(source),
                device_id_type=MESH,
            ).wait_recv()
            return carry

        lax.fori_loop(1, count, landed, 0)
        out_ref[mine] = jnp.sum(held[...], axis=0)

        def send_second(k, carry):
            second(lax.rem(me + k, count)).start()
            return carry

        lax.fori_loop(1, count, send_second, 0)

    def finish(tile, carry):
        @pl.when(tile * stride != me)
        def _():
            first(tile).wait_send()
            pltpu.make_async_remote_copy(
                src_ref=out_ref.at[tile],
                dst_ref=out_ref.at[tile],
                send_sem=send2.at[0],
                recv_sem=recv2.at[tile],
                device_id=where(tile * stride),
                device_id_type=MESH,
            ).wait_recv()

        return carry

    lax.fori_loop(0, tiles, finish, 0)

    @pl.when(owner)
    def _():
        def sent(k, carry):
            second(lax.rem(me + k, count)).wait_send()
            return carry

        lax.fori_loop(1, count, sent, 0)


def reduce_tiles(x, ident):
    tiles = x.shape[0]
    n_row = lax.axis_size("row")
    count = lax.axis_size("grp") * n_row
    return pl.pallas_call(
        functools.partial(reduce_kernel, n_row, count),
        in_specs=[pl.BlockSpec(memory_space=pltpu.VMEM)],
        out_specs=pl.BlockSpec(memory_space=pltpu.VMEM),
        out_shape=jax.ShapeDtypeStruct(x.shape, F32),
        scratch_shapes=[
            pltpu.VMEM((count, 8, 128), F32),
            pltpu.SemaphoreType.DMA((tiles,)),
            pltpu.SemaphoreType.DMA((count,)),
            pltpu.SemaphoreType.DMA((count,)),
            pltpu.SemaphoreType.DMA((tiles,)),
        ],
        compiler_params=pltpu.CompilerParams(collective_id=ident, has_side_effects=True),
        name="reduce_tiles",
    )(x)


def factor_kernel(total, sums_ref, assign_ref, basis_ref, arrived_ref, new_ref, coords_ref, r_ref, m, wb, wa):
    nb = basis_ref.shape[0]
    ns = arrived_ref.shape[0]

    @pl.when(pl.program_id(0) == 0)
    def _():
        scale = 1.0 / total
        placing = (
            lax.broadcasted_iota(jnp.int32, (ns, ns), 0) == assign_ref[...]
        ).astype(F32)
        project = hdot(placing, sums_ref[nb : nb + ns, :] * scale)
        snap = hdot(hdot(placing, sums_ref[nb + ns :, 0:ns] * scale), placing, NT)
        m[0:nb, :] = sums_ref[0:nb, :] * scale
        m[nb : nb + ns, :] = project
        lanes = lax.broadcasted_iota(jnp.int32, (1, nb), 1)
        for k in range(nb):
            block = m[...]
            here = lanes == k
            row = block[k : k + 1, :]
            inv = 1.0 / row[:, k : k + 1]
            row = jnp.where(here, inv, row * inv)
            column = block[:, k : k + 1]
            m[...] = jnp.where(here, 0.0, block) - column * row
            m[k : k + 1, :] = row
        coords = -m[nb : nb + ns, :]
        coords_ref[...] = coords
        schur = snap - hdot(project, coords, NT)
        schur = 0.5 * (schur + hdot_transpose(schur))
        rows = lax.broadcasted_iota(jnp.int32, (ns, ns), 0)
        cols = lax.broadcasted_iota(jnp.int32, (ns, ns), 1)
        left = schur
        right = (rows == cols).astype(F32)
        below = lax.broadcasted_iota(jnp.int32, (ns, 1), 0)
        for k in range(ns):
            factor = left[:, k : k + 1] / left[k : k + 1, k : k + 1]
            factor = jnp.where(below > k, factor, 0.0)
            left, right = left - factor * left[k : k + 1, :], right - factor * right[k : k + 1, :]
        diagonal = jnp.sum(jnp.where(rows == cols, left, 0.0), axis=1, keepdims=True)
        root = 1.0 / jnp.sqrt(diagonal)
        r_ref[...] = jnp.where(cols >= rows, left * root, 0.0)
        inverse = right * root
        wb[...] = -hdot(inverse, coords)
        wa[...] = hdot(inverse, placing)

    bw = jnp.concatenate(split(wb[...]), axis=0)
    aw = jnp.concatenate(split(wa[...]), axis=0)
    bh, bl = split(basis_ref[...])
    ah, al = split(arrived_ref[...])
    out = (bdot(bw, bl, NN) + bdot(aw, al, NN)) + (bdot(bw, bh, NN) + bdot(aw, ah, NN))
    new_ref[...] = out[:ns] + out[ns:]


def hdot_transpose(x):
    n = x.shape[0]
    eye = (
        lax.broadcasted_iota(jnp.int32, (n, n), 0) == lax.broadcasted_iota(jnp.int32, (n, n), 1)
    ).astype(F32)
    return hdot(eye, x, NT)


def factor_and_columns(sums, assignment, basis, arrived, total, chunk):
    nb, rows = basis.shape
    ns = arrived.shape[0]
    whole = lambda i: (0, 0)
    return pl.pallas_call(
        functools.partial(factor_kernel, float(total)),
        grid=(rows // chunk,),
        in_specs=[
            pl.BlockSpec((nb + 2 * ns, nb), whole),
            pl.BlockSpec((1, ns), whole),
            pl.BlockSpec((nb, chunk), lambda i: (0, i)),
            pl.BlockSpec((ns, chunk), lambda i: (0, i)),
        ],
        out_specs=[
            pl.BlockSpec((ns, chunk), lambda i: (0, i)),
            pl.BlockSpec((ns, nb), whole),
            pl.BlockSpec((ns, ns), whole),
        ],
        out_shape=[
            jax.ShapeDtypeStruct((ns, rows), F32),
            jax.ShapeDtypeStruct((ns, nb), F32),
            jax.ShapeDtypeStruct((ns, ns), F32),
        ],
        scratch_shapes=[
            pltpu.VMEM((nb + ns, nb), F32),
            pltpu.VMEM((ns, nb), F32),
            pltpu.VMEM((ns, ns), F32),
        ],
        compiler_params=pltpu.CompilerParams(vmem_limit_bytes=32 << 20),
        name="factor_and_columns",
    )(sums, assignment.reshape(1, ns), basis, arrived)


def apply_kernel(low_ref, mid_ref, high_ref, visc_ref, off_ref, coef_ref, basis_ref, applied_ref, out_ref, ext, bx, nx, sq):
    step = pl.program_id(0)
    ns, chunk = 16, basis_ref.shape[1]
    nb = basis_ref.shape[0]
    terms, slots = coef_ref.shape[0], coef_ref.shape[1]
    width = low_ref.shape[1] // 128
    count = mid_ref.shape[1] // 128
    per_step = chunk // 128

    @pl.when(step == 0)
    def _():
        for b in range(width):
            ext[b] = low_ref[:, b * 128 : (b + 1) * 128]
            ext[width + count + b] = high_ref[:, b * 128 : (b + 1) * 128]
        for b in range(count):
            ext[width + b] = mid_ref[:, b * 128 : (b + 1) * 128]
        bx[...] = jnp.zeros_like(bx)
        nx[...] = jnp.zeros_like(nx)
        sq[...] = jnp.zeros_like(sq)

    lanes = lax.broadcasted_iota(jnp.int32, (slots, 128), 1)

    def one(c, carry):
        first = step * per_step + c
        at = pl.ds(pl.multiple_of(c * 128, 128), 128)
        spot = off_ref[:, at] + (lanes + width * 128)
        low_index = lax.bitwise_and(spot, 127)
        block_index = lax.shift_right_logical(spot, 7)
        totals = [[jnp.zeros((8, 128), F32) for h in range(ns // 8)] for k in range(terms)]
        for t in range(slots):
            lane = jnp.broadcast_to(low_index[t : t + 1, :], (8, 128))
            block = jnp.broadcast_to(block_index[t : t + 1, :], (8, 128))
            picked = [jnp.zeros((8, 128), F32) for h in range(ns // 8)]
            for b in range(2 * width + 1):
                same = block == b
                for h in range(ns // 8):
                    source = ext[first + b, h * 8 : (h + 1) * 8, :]
                    got = jnp.take_along_axis(source, lane, axis=1, mode="promise_in_bounds")
                    picked[h] = jnp.where(same, got, picked[h])
            for k in range(terms):
                weight = coef_ref[k, t : t + 1, at]
                for h in range(ns // 8):
                    totals[k][h] = totals[k][h] + weight * picked[h]
        for k in range(terms):
            for h in range(ns // 8):
                applied_ref[k, h * 8 : (h + 1) * 8, at] = totals[k][h]
        return carry

    lax.fori_loop(0, per_step, one, 0)

    flat = jnp.concatenate([applied_ref[k] for k in range(terms)], axis=0)
    combined = applied_ref[0]
    power = visc_ref[...]
    for k in range(1, terms):
        combined = combined + power * applied_ref[k]
        power = power * visc_ref[...]
    sq[...] += jnp.sum(combined * combined, axis=1, keepdims=True)
    y = jnp.concatenate(split(flat), axis=0)
    x = jnp.concatenate(split(basis_ref[...]), axis=0)
    here = pl.ds(pl.multiple_of(step * chunk, chunk), chunk)
    z = jnp.concatenate(split(mid_ref[:, here]), axis=0)
    bx[...] += bdot(y, x, NT)
    nx[...] += bdot(y, z, NT)

    @pl.when(step == pl.num_programs(0) - 1)
    def _():
        f = terms * ns
        g = bx[...]
        out_ref[0:f, :] = (g[:f, :nb] + g[f:, nb:]) + (g[:f, nb:] + g[f:, :nb])
        s = nx[...]
        out_ref[f : 2 * f, :] = jnp.zeros((f, 128), F32)
        out_ref[f : 2 * f, 0:ns] = (s[:f, :ns] + s[f:, ns:]) + (s[:f, ns:] + s[f:, :ns])
        out_ref[f : f + ns, ns : ns + 1] = sq[...]


def apply_and_blocks(low, new, high, viscosity, offsets, coefs, basis, chunk):
    nb, rows = basis.shape
    ns = new.shape[0]
    terms, slots = coefs.shape[0], coefs.shape[1]
    width = low.shape[1]
    whole = lambda i: (0, 0)
    blocks = (rows + 2 * width) // 128
    return pl.pallas_call(
        apply_kernel,
        grid=(rows // chunk,),
        in_specs=[
            pl.BlockSpec((ns, width), whole),
            pl.BlockSpec((ns, rows), whole),
            pl.BlockSpec((ns, width), whole),
            pl.BlockSpec((ns, 1), whole),
            pl.BlockSpec((slots, chunk), lambda i: (0, i)),
            pl.BlockSpec((terms, slots, chunk), lambda i: (0, 0, i)),
            pl.BlockSpec((nb, chunk), lambda i: (0, i)),
        ],
        out_specs=[
            pl.BlockSpec((terms, ns, chunk), lambda i: (0, 0, i)),
            pl.BlockSpec((2 * terms * ns, nb), whole),
        ],
        out_shape=[
            jax.ShapeDtypeStruct((terms, ns, rows), F32),
            jax.ShapeDtypeStruct((2 * terms * ns, nb), F32),
        ],
        scratch_shapes=[
            pltpu.VMEM((blocks, ns, 128), F32),
            pltpu.VMEM((2 * terms * ns, 2 * nb), F32),
            pltpu.VMEM((2 * terms * ns, 2 * ns), F32),
            pltpu.VMEM((ns, 1), F32),
        ],
        compiler_params=pltpu.CompilerParams(vmem_limit_bytes=32 << 20),
        name="apply_and_blocks",
    )(low, new, high, viscosity, offsets, coefs, basis)


def body(snapshots, basis, assignment, param_index, offsets, coefs):
    ns = assignment.shape[0]
    nb, local = basis.shape
    terms = coefs.shape[0]
    devices = lax.axis_size("grp") * lax.axis_size("row")
    total = local * devices
    width = HALO_BLOCKS * 128
    received = lax.all_to_all(snapshots, "grp", split_axis=1, concat_axis=0, tiled=True)
    arrived = received.reshape(ns, local)
    sums = gram_sums(basis, arrived, 1024)
    sums = reduce_tiles(sums.reshape(-1, 8, nb), 1).reshape(sums.shape)
    new, coords_t, r_factor = factor_and_columns(sums, assignment, basis, arrived, total, 2048)
    forward = [(i, i + 1) for i in range(devices - 1)]
    backward = [(i + 1, i) for i in range(devices - 1)]
    low = lax.ppermute(new[:, local - width :], ("grp", "row"), forward)
    high = lax.ppermute(new[:, :width], ("grp", "row"), backward)
    viscosity = (0.5 + param_index.astype(F32) / NPARAM).reshape(ns, 1)
    applied, parts = apply_and_blocks(low, new, high, viscosity, offsets, coefs, basis, 1024)
    parts = reduce_tiles(parts.reshape(-1, 8, nb), 2).reshape(parts.shape) / total
    f = terms * ns
    blocks = jnp.concatenate([parts[:f], parts[f:, :ns]], axis=1).reshape(terms, ns, nb + ns)
    return (new, applied, coords_t.T, r_factor, blocks.transpose(0, 2, 1), parts[f : f + ns, ns])


def solution(mesh):
    return jax.shard_map(
        body,
        mesh=mesh,
        in_specs=(
            P("grp", None, "row"),
            P(None, ("grp", "row")),
            P(),
            P(),
            P(None, ("grp", "row")),
            P(None, None, ("grp", "row")),
        ),
        out_specs=(P(None, ("grp", "row")), P(None, None, ("grp", "row")), P(), P(), P(), P()),
        check_vma=False,
    )
```

```python
import functools

import jax
import jax.numpy as jnp
from jax import lax
from jax.experimental import pallas as pl
from jax.experimental.pallas import tpu as pltpu
from jax.sharding import PartitionSpec as P

NPARAM = 64
HALO_BLOCKS = 16
F32 = jnp.float32
BF16 = jnp.bfloat16
MESH = pl.DeviceIdType.MESH
NT = (((1,), (1,)), ((), ()))
NN = (((1,), (0,)), ((), ()))


def split(x):
    high = x.astype(BF16)
    low = (x - high.astype(F32)).astype(BF16)
    return high, low


def bdot(a, b, dims):
    return lax.dot_general(a, b, dims, preferred_element_type=F32)


def hdot(a, b, dims=NN):
    return lax.dot_general(a, b, dims, precision=lax.Precision.HIGHEST, preferred_element_type=F32)


def gram_kernel(basis_ref, arrived_ref, out_ref, bb, ab, aa):
    step = pl.program_id(0)

    @pl.when(step == 0)
    def _():
        bb[...] = jnp.zeros_like(bb)
        ab[...] = jnp.zeros_like(ab)
        aa[...] = jnp.zeros_like(aa)

    x = jnp.concatenate(split(basis_ref[...]), axis=0)
    y = jnp.concatenate(split(arrived_ref[...]), axis=0)
    bb[...] += bdot(x, x, NT)
    ab[...] += bdot(y, x, NT)
    aa[...] += bdot(y, y, NT)

    @pl.when(step == pl.num_programs(0) - 1)
    def _():
        nb, ns = basis_ref.shape[0], arrived_ref.shape[0]
        g = bb[...]
        out_ref[0:nb, :] = (g[:nb, :nb] + g[nb:, nb:]) + (g[:nb, nb:] + g[nb:, :nb])
        c = ab[...]
        out_ref[nb : nb + ns, :] = (c[:ns, :nb] + c[ns:, nb:]) + (c[:ns, nb:] + c[ns:, :nb])
        s = aa[...]
        out_ref[nb + ns :, :] = jnp.zeros((out_ref.shape[0] - nb - ns, nb), F32)
        out_ref[nb + ns : nb + 2 * ns, 0:ns] = (s[:ns, :ns] + s[ns:, ns:]) + (s[:ns, ns:] + s[ns:, :ns])


def gram_sums(basis, arrived, chunk):
    nb, rows = basis.shape
    ns = arrived.shape[0]
    height = padded_rows(nb + 2 * ns)
    return pl.pallas_call(
        gram_kernel,
        grid=(rows // chunk,),
        in_specs=[
            pl.BlockSpec((nb, chunk), lambda i: (0, i)),
            pl.BlockSpec((ns, chunk), lambda i: (0, i)),
        ],
        out_specs=pl.BlockSpec((height, nb), lambda i: (0, 0)),
        out_shape=jax.ShapeDtypeStruct((height, nb), F32),
        scratch_shapes=[
            pltpu.VMEM((2 * nb, 2 * nb), F32),
            pltpu.VMEM((2 * ns, 2 * nb), F32),
            pltpu.VMEM((2 * ns, 2 * ns), F32),
        ],
        compiler_params=pltpu.CompilerParams(vmem_limit_bytes=60 << 20),
        name="gram_sums",
    )(basis, arrived)


def exchange_kernel(n_grp, snap_ref, out_ref, ready, held, send_sem, recv_sem):
    me = lax.axis_index("grp")
    row = lax.axis_index("row")
    own = snap_ref.shape[0]
    barrier = pltpu.get_barrier_semaphore()
    for k in range(1, n_grp):
        pl.semaphore_signal(
            barrier, inc=1, device_id=(lax.rem(me + k, n_grp), row), device_id_type=MESH
        )
    for q in range(n_grp):
        ready[q] = snap_ref[:, q, :]
    pl.semaphore_wait(barrier, n_grp - 1)

    def copy(k):
        other = lax.rem(me + k, n_grp)
        return pltpu.make_async_remote_copy(
            src_ref=ready.at[other],
            dst_ref=held.at[k],
            send_sem=send_sem.at[k],
            recv_sem=recv_sem.at[k],
            device_id=(other, row),
            device_id_type=MESH,
        )

    for k in range(1, n_grp):
        copy(k).start()
    held[0] = ready[me]
    for k in range(1, n_grp):
        copy(k).wait()
    for q in range(n_grp):
        out_ref[q * own : (q + 1) * own, :] = held[lax.rem(me - q + n_grp, n_grp)]


def exchange(snapshots):
    own, n_grp, local = snapshots.shape
    return pl.pallas_call(
        functools.partial(exchange_kernel, n_grp),
        in_specs=[pl.BlockSpec(memory_space=pltpu.VMEM)],
        out_specs=pl.BlockSpec(memory_space=pltpu.VMEM),
        out_shape=jax.ShapeDtypeStruct((own * n_grp, local), F32),
        scratch_shapes=[
            pltpu.VMEM((n_grp, own, local), F32),
            pltpu.VMEM((n_grp, own, local), F32),
            pltpu.SemaphoreType.DMA((n_grp,)),
            pltpu.SemaphoreType.DMA((n_grp,)),
        ],
        compiler_params=pltpu.CompilerParams(
            collective_id=3, has_side_effects=True, vmem_limit_bytes=16 << 20
        ),
        name="exchange",
    )(snapshots)


def halo_kernel(n_row, count, new_ref, low_ref, high_ref, send_sem, recv_sem):
    me = lax.axis_index("grp") * n_row + lax.axis_index("row")
    width = low_ref.shape[1]
    local = new_ref.shape[1]
    barrier = pltpu.get_barrier_semaphore()

    def where(device):
        return (device // n_row, lax.rem(device, n_row))

    has_left = me > 0
    has_right = me < count - 1

    for other in (me + 1, me + count - 1):
        pl.semaphore_signal(
            barrier, inc=1, device_id=where(lax.rem(other, count)), device_id_type=MESH
        )
    pl.semaphore_wait(barrier, 2)

    def right():
        return pltpu.make_async_remote_copy(
            src_ref=new_ref.at[:, local - width :],
            dst_ref=low_ref,
            send_sem=send_sem.at[0],
            recv_sem=recv_sem.at[0],
            device_id=where(me + 1),
            device_id_type=MESH,
        )

    def left():
        return pltpu.make_async_remote_copy(
            src_ref=new_ref.at[:, 0:width],
            dst_ref=high_ref,
            send_sem=send_sem.at[1],
            recv_sem=recv_sem.at[1],
            device_id=where(me - 1),
            device_id_type=MESH,
        )

    @pl.when(has_right)
    def _():
        right().start()

    @pl.when(has_left)
    def _():
        left().start()

    @pl.when(jnp.logical_not(has_left))
    def _():
        low_ref[...] = jnp.zeros_like(low_ref)

    @pl.when(jnp.logical_not(has_right))
    def _():
        high_ref[...] = jnp.zeros_like(high_ref)

    @pl.when(has_right)
    def _():
        right().wait_send()
        left().wait_recv()

    @pl.when(has_left)
    def _():
        left().wait_send()
        right().wait_recv()


def halo(new, width):
    n_row = lax.axis_size("row")
    count = lax.axis_size("grp") * n_row
    vmem = pl.BlockSpec(memory_space=pltpu.VMEM)
    side = jax.ShapeDtypeStruct((new.shape[0], width), F32)
    return pl.pallas_call(
        functools.partial(halo_kernel, n_row, count),
        in_specs=[vmem],
        out_specs=[vmem, vmem],
        out_shape=[side, side],
        scratch_shapes=[pltpu.SemaphoreType.DMA((2,)), pltpu.SemaphoreType.DMA((2,))],
        compiler_params=pltpu.CompilerParams(collective_id=4, has_side_effects=True),
        name="halo",
    )(new)


def reduce_kernel(n_grp, n_row, x_ref, out_ref, held, summed, send1, recv1, send2, recv2, send3, recv3):
    mg = lax.axis_index("grp")
    mr = lax.axis_index("row")
    barrier = pltpu.get_barrier_semaphore()

    def greet_row(k, carry):
        pl.semaphore_signal(
            barrier, inc=1, device_id=(mg, lax.rem(mr + k, n_row)), device_id_type=MESH
        )
        return carry

    lax.fori_loop(1, n_row, greet_row, 0)
    for k in range(1, n_grp):
        pl.semaphore_signal(
            barrier, inc=1, device_id=(lax.rem(mg + k, n_grp), mr), device_id_type=MESH
        )
    pl.semaphore_wait(barrier, n_row + n_grp - 2)

    def first(k):
        other = lax.rem(mr + k, n_row)
        return pltpu.make_async_remote_copy(
            src_ref=x_ref.at[other],
            dst_ref=held.at[k],
            send_sem=send1.at[k],
            recv_sem=recv1.at[k],
            device_id=(mg, other),
            device_id_type=MESH,
        )

    def second(k):
        return pltpu.make_async_remote_copy(
            src_ref=summed.at[0],
            dst_ref=summed.at[k],
            send_sem=send2.at[k],
            recv_sem=recv2.at[k],
            device_id=(lax.rem(mg + k, n_grp), mr),
            device_id_type=MESH,
        )

    def third(k, block):
        return pltpu.make_async_remote_copy(
            src_ref=out_ref.at[block],
            dst_ref=out_ref.at[block],
            send_sem=send3.at[k],
            recv_sem=recv3.at[k],
            device_id=(mg, lax.rem(mr + k, n_row)),
            device_id_type=MESH,
        )

    def run(low, high, act):
        def one(k, carry):
            act(k)
            return carry

        lax.fori_loop(low, high, one, 0)

    run(1, n_row, lambda k: first(k).start())
    held[0] = x_ref[mr]
    run(1, n_row, lambda k: first(k).wait_recv())
    summed[0] = jnp.sum(held[...], axis=0)
    run(1, n_grp, lambda k: second(k).start())
    run(1, n_grp, lambda k: second(k).wait())
    total = summed[mg]
    for q in range(1, n_grp):
        total = total + summed[lax.rem(mg + n_grp - q, n_grp)]
    out_ref[mr] = total
    run(1, n_row, lambda k: third(k, mr).start())
    run(1, n_row, lambda k: third(k, lax.rem(mr - k + n_row, n_row)).wait_recv())
    run(1, n_row, lambda k: first(k).wait_send())
    run(1, n_row, lambda k: third(k, mr).wait_send())


def padded_rows(rows):
    step = 8 * lax.axis_size("row")
    return -(-rows // step) * step


def reduce_tiles(x, ident):
    n_row = lax.axis_size("row")
    n_grp = lax.axis_size("grp")
    shape = (n_row, x.shape[0] // n_row, x.shape[1])
    return pl.pallas_call(
        functools.partial(reduce_kernel, n_grp, n_row),
        in_specs=[pl.BlockSpec(memory_space=pltpu.VMEM)],
        out_specs=pl.BlockSpec(memory_space=pltpu.VMEM),
        out_shape=jax.ShapeDtypeStruct(shape, F32),
        scratch_shapes=[
            pltpu.VMEM(shape, F32),
            pltpu.VMEM((n_grp,) + shape[1:], F32),
            pltpu.SemaphoreType.DMA((n_row,)),
            pltpu.SemaphoreType.DMA((n_row,)),
            pltpu.SemaphoreType.DMA((n_grp,)),
            pltpu.SemaphoreType.DMA((n_grp,)),
            pltpu.SemaphoreType.DMA((n_row,)),
            pltpu.SemaphoreType.DMA((n_row,)),
        ],
        compiler_params=pltpu.CompilerParams(collective_id=ident, has_side_effects=True),
        name="reduce_tiles",
    )(x.reshape(shape)).reshape(x.shape)


def factor_kernel(total, sums_ref, assign_ref, basis_ref, arrived_ref, new_ref, coords_ref, r_ref, m, wb, wa):
    nb = basis_ref.shape[0]
    ns = arrived_ref.shape[0]

    @pl.when(pl.program_id(0) == 0)
    def _():
        scale = 1.0 / total
        placing = (
            lax.broadcasted_iota(jnp.int32, (ns, ns), 0) == assign_ref[...]
        ).astype(F32)
        project = hdot(placing, sums_ref[nb : nb + ns, :] * scale)
        snap = hdot(hdot(placing, sums_ref[nb + ns : nb + 2 * ns, 0:ns] * scale), placing, NT)
        m[0:nb, :] = sums_ref[0:nb, :] * scale
        m[nb : nb + ns, :] = project
        lanes = lax.broadcasted_iota(jnp.int32, (1, nb), 1)
        for k in range(nb):
            block = m[...]
            here = lanes == k
            row = block[k : k + 1, :]
            inv = 1.0 / row[:, k : k + 1]
            row = jnp.where(here, inv, row * inv)
            column = block[:, k : k + 1]
            m[...] = jnp.where(here, 0.0, block) - column * row
            m[k : k + 1, :] = row
        coords = -m[nb : nb + ns, :]
        coords_ref[...] = coords
        schur = snap - hdot(project, coords, NT)
        schur = 0.5 * (schur + hdot_transpose(schur))
        rows = lax.broadcasted_iota(jnp.int32, (ns, ns), 0)
        cols = lax.broadcasted_iota(jnp.int32, (ns, ns), 1)
        left = schur
        right = (rows == cols).astype(F32)
        below = lax.broadcasted_iota(jnp.int32, (ns, 1), 0)
        for k in range(ns):
            factor = left[:, k : k + 1] / left[k : k + 1, k : k + 1]
            factor = jnp.where(below > k, factor, 0.0)
            left, right = left - factor * left[k : k + 1, :], right - factor * right[k : k + 1, :]
        diagonal = jnp.sum(jnp.where(rows == cols, left, 0.0), axis=1, keepdims=True)
        root = 1.0 / jnp.sqrt(diagonal)
        r_ref[...] = jnp.where(cols >= rows, left * root, 0.0)
        inverse = right * root
        wb[...] = -hdot(inverse, coords)
        wa[...] = hdot(inverse, placing)

    bw = jnp.concatenate(split(wb[...]), axis=0)
    aw = jnp.concatenate(split(wa[...]), axis=0)
    bh, bl = split(basis_ref[...])
    ah, al = split(arrived_ref[...])
    out = (bdot(bw, bl, NN) + bdot(aw, al, NN)) + (bdot(bw, bh, NN) + bdot(aw, ah, NN))
    new_ref[...] = out[:ns] + out[ns:]


def hdot_transpose(x):
    n = x.shape[0]
    eye = (
        lax.broadcasted_iota(jnp.int32, (n, n), 0) == lax.broadcasted_iota(jnp.int32, (n, n), 1)
    ).astype(F32)
    return hdot(eye, x, NT)


def factor_and_columns(sums, assignment, basis, arrived, total, chunk):
    nb, rows = basis.shape
    ns = arrived.shape[0]
    whole = lambda i: (0, 0)
    return pl.pallas_call(
        functools.partial(factor_kernel, float(total)),
        grid=(rows // chunk,),
        in_specs=[
            pl.BlockSpec(sums.shape, whole),
            pl.BlockSpec((1, ns), whole),
            pl.BlockSpec((nb, chunk), lambda i: (0, i)),
            pl.BlockSpec((ns, chunk), lambda i: (0, i)),
        ],
        out_specs=[
            pl.BlockSpec((ns, chunk), lambda i: (0, i)),
            pl.BlockSpec((ns, nb), whole),
            pl.BlockSpec((ns, ns), whole),
        ],
        out_shape=[
            jax.ShapeDtypeStruct((ns, rows), F32),
            jax.ShapeDtypeStruct((ns, nb), F32),
            jax.ShapeDtypeStruct((ns, ns), F32),
        ],
        scratch_shapes=[
            pltpu.VMEM((nb + ns, nb), F32),
            pltpu.VMEM((ns, nb), F32),
            pltpu.VMEM((ns, ns), F32),
        ],
        compiler_params=pltpu.CompilerParams(vmem_limit_bytes=60 << 20),
        name="factor_and_columns",
    )(sums, assignment.reshape(1, ns), basis, arrived)


def apply_kernel(low_ref, mid_ref, high_ref, visc_ref, off_ref, coef_ref, basis_ref, applied_ref, out_ref, ext, bx, nx, sq):
    step = pl.program_id(0)
    ns, chunk = 16, basis_ref.shape[1]
    nb = basis_ref.shape[0]
    terms, slots = coef_ref.shape[0], coef_ref.shape[1]
    width = low_ref.shape[1] // 128
    count = mid_ref.shape[1] // 128
    per_step = chunk // 128

    @pl.when(step == 0)
    def _():
        for b in range(width):
            ext[b] = low_ref[:, b * 128 : (b + 1) * 128]
            ext[width + count + b] = high_ref[:, b * 128 : (b + 1) * 128]
        for b in range(count):
            ext[width + b] = mid_ref[:, b * 128 : (b + 1) * 128]
        bx[...] = jnp.zeros_like(bx)
        nx[...] = jnp.zeros_like(nx)
        sq[...] = jnp.zeros_like(sq)

    lanes = lax.broadcasted_iota(jnp.int32, (slots, 128), 1)

    def one(c, carry):
        first = step * per_step + c
        at = pl.ds(pl.multiple_of(c * 128, 128), 128)
        spot = off_ref[:, at] + (lanes + width * 128)
        low_index = lax.bitwise_and(spot, 127)
        block_index = lax.shift_right_logical(spot, 7)
        totals = [[jnp.zeros((8, 128), F32) for h in range(ns // 8)] for k in range(terms)]
        for t in range(slots):
            lane = jnp.broadcast_to(low_index[t : t + 1, :], (8, 128))
            block = jnp.broadcast_to(block_index[t : t + 1, :], (8, 128))
            picked = [jnp.zeros((8, 128), F32) for h in range(ns // 8)]
            for b in range(2 * width + 1):
                same = block == b
                for h in range(ns // 8):
                    source = ext[first + b, h * 8 : (h + 1) * 8, :]
                    got = jnp.take_along_axis(source, lane, axis=1, mode="promise_in_bounds")
                    picked[h] = jnp.where(same, got, picked[h])
            for k in range(terms):
                weight = coef_ref[k, t : t + 1, at]
                for h in range(ns // 8):
                    totals[k][h] = totals[k][h] + weight * picked[h]
        for k in range(terms):
            for h in range(ns // 8):
                applied_ref[k, h * 8 : (h + 1) * 8, at] = totals[k][h]
        return carry

    lax.fori_loop(0, per_step, one, 0)

    flat = jnp.concatenate([applied_ref[k] for k in range(terms)], axis=0)
    combined = applied_ref[0]
    power = visc_ref[...]
    for k in range(1, terms):
        combined = combined + power * applied_ref[k]
        power = power * visc_ref[...]
    sq[...] += jnp.sum(combined * combined, axis=1, keepdims=True)
    y = jnp.concatenate(split(flat), axis=0)
    x = jnp.concatenate(split(basis_ref[...]), axis=0)
    here = pl.ds(pl.multiple_of(step * chunk, chunk), chunk)
    z = jnp.concatenate(split(mid_ref[:, here]), axis=0)
    bx[...] += bdot(y, x, NT)
    nx[...] += bdot(y, z, NT)

    @pl.when(step == pl.num_programs(0) - 1)
    def _():
        f = terms * ns
        g = bx[...]
        out_ref[0:f, :] = (g[:f, :nb] + g[f:, nb:]) + (g[:f, nb:] + g[f:, :nb])
        s = nx[...]
        out_ref[f:, :] = jnp.zeros((out_ref.shape[0] - f, nb), F32)
        out_ref[f : 2 * f, 0:ns] = (s[:f, :ns] + s[f:, ns:]) + (s[:f, ns:] + s[f:, :ns])
        out_ref[f : f + ns, ns : ns + 1] = sq[...]


def apply_and_blocks(low, new, high, viscosity, offsets, coefs, basis, chunk):
    nb, rows = basis.shape
    ns = new.shape[0]
    terms, slots = coefs.shape[0], coefs.shape[1]
    width = low.shape[1]
    whole = lambda i: (0, 0)
    blocks = (rows + 2 * width) // 128
    height = padded_rows(2 * terms * ns)
    return pl.pallas_call(
        apply_kernel,
        grid=(rows // chunk,),
        in_specs=[
            pl.BlockSpec((ns, width), whole),
            pl.BlockSpec((ns, rows), whole),
            pl.BlockSpec((ns, width), whole),
            pl.BlockSpec((ns, 1), whole),
            pl.BlockSpec((slots, chunk), lambda i: (0, i)),
            pl.BlockSpec((terms, slots, chunk), lambda i: (0, 0, i)),
            pl.BlockSpec((nb, chunk), lambda i: (0, i)),
        ],
        out_specs=[
            pl.BlockSpec((terms, ns, chunk), lambda i: (0, 0, i)),
            pl.BlockSpec((height, nb), whole),
        ],
        out_shape=[
            jax.ShapeDtypeStruct((terms, ns, rows), F32),
            jax.ShapeDtypeStruct((height, nb), F32),
        ],
        scratch_shapes=[
            pltpu.VMEM((blocks, ns, 128), F32),
            pltpu.VMEM((2 * terms * ns, 2 * nb), F32),
            pltpu.VMEM((2 * terms * ns, 2 * ns), F32),
            pltpu.VMEM((ns, 1), F32),
        ],
        compiler_params=pltpu.CompilerParams(vmem_limit_bytes=60 << 20),
        name="apply_and_blocks",
    )(low, new, high, viscosity, offsets, coefs, basis)


def body(snapshots, basis, assignment, param_index, offsets, coefs):
    ns = assignment.shape[0]
    nb, local = basis.shape
    terms = coefs.shape[0]
    devices = lax.axis_size("grp") * lax.axis_size("row")
    total = local * devices
    width = HALO_BLOCKS * 128
    arrived = exchange(snapshots)
    sums = reduce_tiles(gram_sums(basis, arrived, 1024), 1)
    new, coords_t, r_factor = factor_and_columns(sums, assignment, basis, arrived, total, 2048)
    low, high = halo(new, width)
    viscosity = (0.5 + param_index.astype(F32) / NPARAM).reshape(ns, 1)
    applied, parts = apply_and_blocks(low, new, high, viscosity, offsets, coefs, basis, 1024)
    parts = reduce_tiles(parts, 2) / total
    f = terms * ns
    blocks = jnp.concatenate([parts[:f], parts[f : 2 * f, :ns]], axis=1).reshape(terms, ns, nb + ns)
    return (new, applied, coords_t.T, r_factor, blocks.transpose(0, 2, 1), parts[f : f + ns, ns])


def solution(mesh):
    return jax.shard_map(
        body,
        mesh=mesh,
        in_specs=(
            P("grp", None, "row"),
            P(None, ("grp", "row")),
            P(),
            P(),
            P(None, ("grp", "row")),
            P(None, None, ("grp", "row")),
        ),
        out_specs=(P(None, ("grp", "row")), P(None, None, ("grp", "row")), P(), P(), P(), P()),
        check_vma=False,
    )
```

```python
import functools

import jax
import jax.numpy as jnp
from jax import lax
from jax.experimental import pallas as pl
from jax.experimental.pallas import tpu as pltpu
from jax.sharding import PartitionSpec as P

NPARAM = 64
HALO_BLOCKS = 16
LANE_SLOTS = 3
F32 = jnp.float32
BF16 = jnp.bfloat16
MESH = pl.DeviceIdType.MESH
NT = (((1,), (1,)), ((), ()))
NN = (((1,), (0,)), ((), ()))


def split(x):
    high = x.astype(BF16)
    low = (x - high.astype(F32)).astype(BF16)
    return high, low


def bdot(a, b, dims):
    return lax.dot_general(a, b, dims, preferred_element_type=F32)


def hdot(a, b, dims=NN):
    return lax.dot_general(a, b, dims, precision=lax.Precision.HIGHEST, preferred_element_type=F32)


def gram_kernel(basis_ref, arrived_ref, out_ref, bb, ab, aa):
    step = pl.program_id(0)

    @pl.when(step == 0)
    def _():
        bb[...] = jnp.zeros_like(bb)
        ab[...] = jnp.zeros_like(ab)
        aa[...] = jnp.zeros_like(aa)

    x = jnp.concatenate(split(basis_ref[...]), axis=0)
    y = jnp.concatenate(split(arrived_ref[...]), axis=0)
    bb[...] += bdot(x, x, NT)
    ab[...] += bdot(y, x, NT)
    aa[...] += bdot(y, y, NT)

    @pl.when(step == pl.num_programs(0) - 1)
    def _():
        nb, ns = basis_ref.shape[0], arrived_ref.shape[0]
        g = bb[...]
        out_ref[0:nb, :] = (g[:nb, :nb] + g[nb:, nb:]) + (g[:nb, nb:] + g[nb:, :nb])
        c = ab[...]
        out_ref[nb : nb + ns, :] = (c[:ns, :nb] + c[ns:, nb:]) + (c[:ns, nb:] + c[ns:, :nb])
        s = aa[...]
        out_ref[nb + ns :, :] = jnp.zeros((out_ref.shape[0] - nb - ns, nb), F32)
        out_ref[nb + ns : nb + 2 * ns, 0:ns] = (s[:ns, :ns] + s[ns:, ns:]) + (s[:ns, ns:] + s[ns:, :ns])


def gram_sums(basis, arrived, chunk):
    nb, rows = basis.shape
    ns = arrived.shape[0]
    height = padded_rows(nb + 2 * ns)
    return pl.pallas_call(
        gram_kernel,
        grid=(rows // chunk,),
        in_specs=[
            pl.BlockSpec((nb, chunk), lambda i: (0, i)),
            pl.BlockSpec((ns, chunk), lambda i: (0, i)),
        ],
        out_specs=pl.BlockSpec((height, nb), lambda i: (0, 0)),
        out_shape=jax.ShapeDtypeStruct((height, nb), F32),
        scratch_shapes=[
            pltpu.VMEM((2 * nb, 2 * nb), F32),
            pltpu.VMEM((2 * ns, 2 * nb), F32),
            pltpu.VMEM((2 * ns, 2 * ns), F32),
        ],
        compiler_params=pltpu.CompilerParams(vmem_limit_bytes=60 << 20),
        name="gram_sums",
    )(basis, arrived)


def exchange_kernel(n_grp, snap_ref, out_ref, ready, held, send_sem, recv_sem):
    me = lax.axis_index("grp")
    row = lax.axis_index("row")
    own = snap_ref.shape[0]
    barrier = pltpu.get_barrier_semaphore()
    for k in range(1, n_grp):
        pl.semaphore_signal(
            barrier, inc=1, device_id=(lax.rem(me + k, n_grp), row), device_id_type=MESH
        )
    for q in range(n_grp):
        ready[q] = snap_ref[:, q, :]
    pl.semaphore_wait(barrier, n_grp - 1)

    def copy(k):
        other = lax.rem(me + k, n_grp)
        return pltpu.make_async_remote_copy(
            src_ref=ready.at[other],
            dst_ref=held.at[k],
            send_sem=send_sem.at[k],
            recv_sem=recv_sem.at[k],
            device_id=(other, row),
            device_id_type=MESH,
        )

    for k in range(1, n_grp):
        copy(k).start()
    held[0] = ready[me]
    for k in range(1, n_grp):
        copy(k).wait()
    for q in range(n_grp):
        out_ref[q * own : (q + 1) * own, :] = held[lax.rem(me - q + n_grp, n_grp)]


def exchange(snapshots):
    own, n_grp, local = snapshots.shape
    return pl.pallas_call(
        functools.partial(exchange_kernel, n_grp),
        in_specs=[pl.BlockSpec(memory_space=pltpu.VMEM)],
        out_specs=pl.BlockSpec(memory_space=pltpu.VMEM),
        out_shape=jax.ShapeDtypeStruct((own * n_grp, local), F32),
        scratch_shapes=[
            pltpu.VMEM((n_grp, own, local), F32),
            pltpu.VMEM((n_grp, own, local), F32),
            pltpu.SemaphoreType.DMA((n_grp,)),
            pltpu.SemaphoreType.DMA((n_grp,)),
        ],
        compiler_params=pltpu.CompilerParams(
            collective_id=3, has_side_effects=True, vmem_limit_bytes=16 << 20
        ),
        name="exchange",
    )(snapshots)


def halo_kernel(n_row, count, new_ref, low_ref, high_ref, send_sem, recv_sem):
    me = lax.axis_index("grp") * n_row + lax.axis_index("row")
    width = low_ref.shape[1]
    local = new_ref.shape[1]
    barrier = pltpu.get_barrier_semaphore()

    def where(device):
        return (device // n_row, lax.rem(device, n_row))

    has_left = me > 0
    has_right = me < count - 1

    for other in (me + 1, me + count - 1):
        pl.semaphore_signal(
            barrier, inc=1, device_id=where(lax.rem(other, count)), device_id_type=MESH
        )
    pl.semaphore_wait(barrier, 2)

    def right():
        return pltpu.make_async_remote_copy(
            src_ref=new_ref.at[:, local - width :],
            dst_ref=low_ref,
            send_sem=send_sem.at[0],
            recv_sem=recv_sem.at[0],
            device_id=where(me + 1),
            device_id_type=MESH,
        )

    def left():
        return pltpu.make_async_remote_copy(
            src_ref=new_ref.at[:, 0:width],
            dst_ref=high_ref,
            send_sem=send_sem.at[1],
            recv_sem=recv_sem.at[1],
            device_id=where(me - 1),
            device_id_type=MESH,
        )

    @pl.when(has_right)
    def _():
        right().start()

    @pl.when(has_left)
    def _():
        left().start()

    @pl.when(jnp.logical_not(has_left))
    def _():
        low_ref[...] = jnp.zeros_like(low_ref)

    @pl.when(jnp.logical_not(has_right))
    def _():
        high_ref[...] = jnp.zeros_like(high_ref)

    @pl.when(has_right)
    def _():
        right().wait_send()
        left().wait_recv()

    @pl.when(has_left)
    def _():
        left().wait_send()
        right().wait_recv()


def halo(new, width):
    n_row = lax.axis_size("row")
    count = lax.axis_size("grp") * n_row
    vmem = pl.BlockSpec(memory_space=pltpu.VMEM)
    side = jax.ShapeDtypeStruct((new.shape[0], width), F32)
    return pl.pallas_call(
        functools.partial(halo_kernel, n_row, count),
        in_specs=[vmem],
        out_specs=[vmem, vmem],
        out_shape=[side, side],
        scratch_shapes=[pltpu.SemaphoreType.DMA((2,)), pltpu.SemaphoreType.DMA((2,))],
        compiler_params=pltpu.CompilerParams(collective_id=4, has_side_effects=True),
        name="halo",
    )(new)


def reduce_kernel(n_grp, n_row, x_ref, out_ref, held, summed, send1, recv1, send2, recv2, send3, recv3):
    mg = lax.axis_index("grp")
    mr = lax.axis_index("row")
    barrier = pltpu.get_barrier_semaphore()

    def greet_row(k, carry):
        pl.semaphore_signal(
            barrier, inc=1, device_id=(mg, lax.rem(mr + k, n_row)), device_id_type=MESH
        )
        return carry

    lax.fori_loop(1, n_row, greet_row, 0)
    for k in range(1, n_grp):
        pl.semaphore_signal(
            barrier, inc=1, device_id=(lax.rem(mg + k, n_grp), mr), device_id_type=MESH
        )
    pl.semaphore_wait(barrier, n_row + n_grp - 2)

    def first(k):
        other = lax.rem(mr + k, n_row)
        return pltpu.make_async_remote_copy(
            src_ref=x_ref.at[other],
            dst_ref=held.at[k],
            send_sem=send1.at[k],
            recv_sem=recv1.at[k],
            device_id=(mg, other),
            device_id_type=MESH,
        )

    def second(k):
        return pltpu.make_async_remote_copy(
            src_ref=summed.at[0],
            dst_ref=summed.at[k],
            send_sem=send2.at[k],
            recv_sem=recv2.at[k],
            device_id=(lax.rem(mg + k, n_grp), mr),
            device_id_type=MESH,
        )

    def third(k, block):
        return pltpu.make_async_remote_copy(
            src_ref=out_ref.at[block],
            dst_ref=out_ref.at[block],
            send_sem=send3.at[k],
            recv_sem=recv3.at[k],
            device_id=(mg, lax.rem(mr + k, n_row)),
            device_id_type=MESH,
        )

    def run(low, high, act):
        def one(k, carry):
            act(k)
            return carry

        lax.fori_loop(low, high, one, 0)

    run(1, n_row, lambda k: first(k).start())
    held[0] = x_ref[mr]
    run(1, n_row, lambda k: first(k).wait_recv())
    summed[0] = jnp.sum(held[...], axis=0)
    run(1, n_grp, lambda k: second(k).start())
    run(1, n_grp, lambda k: second(k).wait())
    total = summed[mg]
    for q in range(1, n_grp):
        total = total + summed[lax.rem(mg + n_grp - q, n_grp)]
    out_ref[mr] = total
    run(1, n_row, lambda k: third(k, mr).start())
    run(1, n_row, lambda k: third(k, lax.rem(mr - k + n_row, n_row)).wait_recv())
    run(1, n_row, lambda k: first(k).wait_send())
    run(1, n_row, lambda k: third(k, mr).wait_send())


def padded_rows(rows):
    step = 8 * lax.axis_size("row")
    return -(-rows // step) * step


def reduce_tiles(x, ident):
    n_row = lax.axis_size("row")
    n_grp = lax.axis_size("grp")
    shape = (n_row, x.shape[0] // n_row, x.shape[1])
    return pl.pallas_call(
        functools.partial(reduce_kernel, n_grp, n_row),
        in_specs=[pl.BlockSpec(memory_space=pltpu.VMEM)],
        out_specs=pl.BlockSpec(memory_space=pltpu.VMEM),
        out_shape=jax.ShapeDtypeStruct(shape, F32),
        scratch_shapes=[
            pltpu.VMEM(shape, F32),
            pltpu.VMEM((n_grp,) + shape[1:], F32),
            pltpu.SemaphoreType.DMA((n_row,)),
            pltpu.SemaphoreType.DMA((n_row,)),
            pltpu.SemaphoreType.DMA((n_grp,)),
            pltpu.SemaphoreType.DMA((n_grp,)),
            pltpu.SemaphoreType.DMA((n_row,)),
            pltpu.SemaphoreType.DMA((n_row,)),
        ],
        compiler_params=pltpu.CompilerParams(collective_id=ident, has_side_effects=True),
        name="reduce_tiles",
    )(x.reshape(shape)).reshape(x.shape)


def factor_kernel(total, sums_ref, assign_ref, basis_ref, arrived_ref, new_ref, coords_ref, r_ref, m, wb, wa):
    nb = basis_ref.shape[0]
    ns = arrived_ref.shape[0]

    @pl.when(pl.program_id(0) == 0)
    def _():
        scale = 1.0 / total
        placing = (
            lax.broadcasted_iota(jnp.int32, (ns, ns), 0) == assign_ref[...]
        ).astype(F32)
        project = hdot(placing, sums_ref[nb : nb + ns, :] * scale)
        snap = hdot(hdot(placing, sums_ref[nb + ns : nb + 2 * ns, 0:ns] * scale), placing, NT)
        m[0:nb, :] = sums_ref[0:nb, :] * scale
        m[nb : nb + ns, :] = project
        lanes = lax.broadcasted_iota(jnp.int32, (1, nb), 1)
        for k in range(nb):
            block = m[...]
            here = lanes == k
            row = block[k : k + 1, :]
            inv = 1.0 / row[:, k : k + 1]
            row = jnp.where(here, inv, row * inv)
            column = block[:, k : k + 1]
            m[...] = jnp.where(here, 0.0, block) - column * row
            m[k : k + 1, :] = row
        coords = -m[nb : nb + ns, :]
        coords_ref[...] = coords
        schur = snap - hdot(project, coords, NT)
        schur = 0.5 * (schur + hdot_transpose(schur))
        rows = lax.broadcasted_iota(jnp.int32, (ns, ns), 0)
        cols = lax.broadcasted_iota(jnp.int32, (ns, ns), 1)
        left = schur
        right = (rows == cols).astype(F32)
        below = lax.broadcasted_iota(jnp.int32, (ns, 1), 0)
        for k in range(ns):
            factor = left[:, k : k + 1] / left[k : k + 1, k : k + 1]
            factor = jnp.where(below > k, factor, 0.0)
            left, right = left - factor * left[k : k + 1, :], right - factor * right[k : k + 1, :]
        diagonal = jnp.sum(jnp.where(rows == cols, left, 0.0), axis=1, keepdims=True)
        root = 1.0 / jnp.sqrt(diagonal)
        r_ref[...] = jnp.where(cols >= rows, left * root, 0.0)
        inverse = right * root
        wb[...] = -hdot(inverse, coords)
        wa[...] = hdot(inverse, placing)

    bw = jnp.concatenate(split(wb[...]), axis=0)
    aw = jnp.concatenate(split(wa[...]), axis=0)
    bh, bl = split(basis_ref[...])
    ah, al = split(arrived_ref[...])
    out = (bdot(bw, bl, NN) + bdot(aw, al, NN)) + (bdot(bw, bh, NN) + bdot(aw, ah, NN))
    new_ref[...] = out[:ns] + out[ns:]


def hdot_transpose(x):
    n = x.shape[0]
    eye = (
        lax.broadcasted_iota(jnp.int32, (n, n), 0) == lax.broadcasted_iota(jnp.int32, (n, n), 1)
    ).astype(F32)
    return hdot(eye, x, NT)


def factor_and_columns(sums, assignment, basis, arrived, total, chunk):
    nb, rows = basis.shape
    ns = arrived.shape[0]
    whole = lambda i: (0, 0)
    return pl.pallas_call(
        functools.partial(factor_kernel, float(total)),
        grid=(rows // chunk,),
        in_specs=[
            pl.BlockSpec(sums.shape, whole),
            pl.BlockSpec((1, ns), whole),
            pl.BlockSpec((nb, chunk), lambda i: (0, i)),
            pl.BlockSpec((ns, chunk), lambda i: (0, i)),
        ],
        out_specs=[
            pl.BlockSpec((ns, chunk), lambda i: (0, i)),
            pl.BlockSpec((ns, nb), whole),
            pl.BlockSpec((ns, ns), whole),
        ],
        out_shape=[
            jax.ShapeDtypeStruct((ns, rows), F32),
            jax.ShapeDtypeStruct((ns, nb), F32),
            jax.ShapeDtypeStruct((ns, ns), F32),
        ],
        scratch_shapes=[
            pltpu.VMEM((nb + ns, nb), F32),
            pltpu.VMEM((ns, nb), F32),
            pltpu.VMEM((ns, ns), F32),
        ],
        compiler_params=pltpu.CompilerParams(vmem_limit_bytes=60 << 20),
        name="factor_and_columns",
    )(sums, assignment.reshape(1, ns), basis, arrived)


def apply_kernel(low_ref, mid_ref, high_ref, visc_ref, off_ref, coef_ref, basis_ref, applied_ref, out_ref, ext, wide, bx, nx, sq):
    step = pl.program_id(0)
    ns, chunk = 16, basis_ref.shape[1]
    nb = basis_ref.shape[0]
    terms, slots = coef_ref.shape[0], coef_ref.shape[1]
    width = low_ref.shape[1] // 128
    count = mid_ref.shape[1] // 128
    per_step = chunk // 256
    halves = ns // 8

    @pl.when(step == 0)
    def _():
        for b in range(width):
            ext[b] = low_ref[:, b * 128 : (b + 1) * 128]
            ext[width + count + b] = high_ref[:, b * 128 : (b + 1) * 128]
        for b in range(count):
            ext[width + b] = mid_ref[:, b * 128 : (b + 1) * 128]
        for ref, start in ((low_ref, 0), (mid_ref, width // 2), (high_ref, (width + count) // 2)):
            for b in range(ref.shape[1] // 256):
                wide[start + b] = jnp.concatenate(split(ref[:, b * 256 : (b + 1) * 256]), axis=0)
        bx[...] = jnp.zeros_like(bx)
        nx[...] = jnp.zeros_like(nx)
        sq[...] = jnp.zeros_like(sq)

    lanes = lax.broadcasted_iota(jnp.int32, (slots, 256), 1)
    depth = lax.broadcasted_iota(jnp.int32, (256, 256), 0)

    def by_lanes(spot, t, first):
        low_index = lax.bitwise_and(spot, 127)
        block_index = lax.shift_right_logical(spot, 7)
        sides = [[] for h in range(halves)]
        for u in range(2):
            part = slice(u * 128, (u + 1) * 128)
            lane = jnp.broadcast_to(low_index[t : t + 1, part], (8, 128))
            block = jnp.broadcast_to(block_index[t : t + 1, part] - u, (8, 128))
            picked = [jnp.zeros((8, 128), F32) for h in range(halves)]
            for b in range(2 * width + 1):
                same = block == b
                for h in range(halves):
                    source = ext[2 * first + u + b, h * 8 : (h + 1) * 8, :]
                    got = jnp.take_along_axis(source, lane, axis=1, mode="promise_in_bounds")
                    picked[h] = jnp.where(same, got, picked[h])
            for h in range(halves):
                sides[h].append(picked[h])
        return [jnp.concatenate(side, axis=1) for side in sides]

    def by_product(spot, t, window):
        low_index = lax.bitwise_and(spot, 255)
        block = jnp.broadcast_to(lax.shift_right_logical(spot, 8)[t : t + 1, :], (8, 256))
        chosen = (depth == low_index[t : t + 1, :]).astype(F32).astype(BF16)
        found = jnp.dot(window, chosen, preferred_element_type=F32)
        picked = [found[g * 8 : (g + 1) * 8, :] for g in range(2 * halves)]
        for b in range(1, width + 1):
            same = block == b
            for g in range(2 * halves):
                at = b * 2 * ns + g * 8
                picked[g] = jnp.where(same, found[at : at + 8, :], picked[g])
        return [picked[h] + picked[halves + h] for h in range(halves)]

    def one(c, carry):
        first = step * per_step + c
        at = pl.ds(pl.multiple_of(c * 256, 256), 256)
        spot = off_ref[:, at] + (lanes + width * 128)
        window = wide[pl.ds(first, width + 1)].reshape((width + 1) * 2 * ns, 256)
        totals = [[jnp.zeros((8, 256), F32) for h in range(halves)] for k in range(terms)]
        for t in range(slots):
            if t < LANE_SLOTS:
                picked = by_lanes(spot, t, first)
            else:
                picked = by_product(spot, t, window)
            for k in range(terms):
                weight = coef_ref[k, t : t + 1, at]
                for h in range(halves):
                    totals[k][h] = totals[k][h] + weight * picked[h]
        for k in range(terms):
            for h in range(halves):
                applied_ref[k, h * 8 : (h + 1) * 8, at] = totals[k][h]
        return carry

    lax.fori_loop(0, per_step, one, 0)

    flat = jnp.concatenate([applied_ref[k] for k in range(terms)], axis=0)
    combined = applied_ref[0]
    power = visc_ref[...]
    for k in range(1, terms):
        combined = combined + power * applied_ref[k]
        power = power * visc_ref[...]
    sq[...] += jnp.sum(combined * combined, axis=1, keepdims=True)
    y = jnp.concatenate(split(flat), axis=0)
    x = jnp.concatenate(split(basis_ref[...]), axis=0)
    here = pl.ds(pl.multiple_of(step * chunk, chunk), chunk)
    z = jnp.concatenate(split(mid_ref[:, here]), axis=0)
    bx[...] += bdot(y, x, NT)
    nx[...] += bdot(y, z, NT)

    @pl.when(step == pl.num_programs(0) - 1)
    def _():
        f = terms * ns
        g = bx[...]
        out_ref[0:f, :] = (g[:f, :nb] + g[f:, nb:]) + (g[:f, nb:] + g[f:, :nb])
        s = nx[...]
        out_ref[f:, :] = jnp.zeros((out_ref.shape[0] - f, nb), F32)
        out_ref[f : 2 * f, 0:ns] = (s[:f, :ns] + s[f:, ns:]) + (s[:f, ns:] + s[f:, :ns])
        out_ref[f : f + ns, ns : ns + 1] = sq[...]


def apply_and_blocks(low, new, high, viscosity, offsets, coefs, basis, chunk):
    nb, rows = basis.shape
    ns = new.shape[0]
    terms, slots = coefs.shape[0], coefs.shape[1]
    width = low.shape[1]
    whole = lambda i: (0, 0)
    blocks = (rows + 2 * width) // 128
    height = padded_rows(2 * terms * ns)
    return pl.pallas_call(
        apply_kernel,
        grid=(rows // chunk,),
        in_specs=[
            pl.BlockSpec((ns, width), whole),
            pl.BlockSpec((ns, rows), whole),
            pl.BlockSpec((ns, width), whole),
            pl.BlockSpec((ns, 1), whole),
            pl.BlockSpec((slots, chunk), lambda i: (0, i)),
            pl.BlockSpec((terms, slots, chunk), lambda i: (0, 0, i)),
            pl.BlockSpec((nb, chunk), lambda i: (0, i)),
        ],
        out_specs=[
            pl.BlockSpec((terms, ns, chunk), lambda i: (0, 0, i)),
            pl.BlockSpec((height, nb), whole),
        ],
        out_shape=[
            jax.ShapeDtypeStruct((terms, ns, rows), F32),
            jax.ShapeDtypeStruct((height, nb), F32),
        ],
        scratch_shapes=[
            pltpu.VMEM((blocks, ns, 128), F32),
            pltpu.VMEM((blocks // 2, 2 * ns, 256), BF16),
            pltpu.VMEM((2 * terms * ns, 2 * nb), F32),
            pltpu.VMEM((2 * terms * ns, 2 * ns), F32),
            pltpu.VMEM((ns, 1), F32),
        ],
        compiler_params=pltpu.CompilerParams(vmem_limit_bytes=60 << 20),
        name="apply_and_blocks",
    )(low, new, high, viscosity, offsets, coefs, basis)


def body(snapshots, basis, assignment, param_index, offsets, coefs):
    ns = assignment.shape[0]
    nb, local = basis.shape
    terms = coefs.shape[0]
    devices = lax.axis_size("grp") * lax.axis_size("row")
    total = local * devices
    width = HALO_BLOCKS * 128
    arrived = exchange(snapshots)
    sums = reduce_tiles(gram_sums(basis, arrived, 1024), 1)
    new, coords_t, r_factor = factor_and_columns(sums, assignment, basis, arrived, total, 2048)
    low, high = halo(new, width)
    viscosity = (0.5 + param_index.astype(F32) / NPARAM).reshape(ns, 1)
    applied, parts = apply_and_blocks(low, new, high, viscosity, offsets, coefs, basis, 1024)
    parts = reduce_tiles(parts, 2) / total
    f = terms * ns
    blocks = jnp.concatenate([parts[:f], parts[f : 2 * f, :ns]], axis=1).reshape(terms, ns, nb + ns)
    return (new, applied, coords_t.T, r_factor, blocks.transpose(0, 2, 1), parts[f : f + ns, ns])


def solution(mesh):
    return jax.shard_map(
        body,
        mesh=mesh,
        in_specs=(
            P("grp", None, "row"),
            P(None, ("grp", "row")),
            P(),
            P(),
            P(None, ("grp", "row")),
            P(None, None, ("grp", "row")),
        ),
        out_specs=(P(None, ("grp", "row")), P(None, None, ("grp", "row")), P(), P(), P(), P()),
        check_vma=False,
    )
```

```python
import functools

import jax
import jax.numpy as jnp
from jax import lax
from jax.experimental import pallas as pl
from jax.experimental.pallas import tpu as pltpu
from jax.sharding import PartitionSpec as P

NPARAM = 64
HALO_BLOCKS = 16
LANE_SLOTS = 3
F32 = jnp.float32
BF16 = jnp.bfloat16
MESH = pl.DeviceIdType.MESH
NT = (((1,), (1,)), ((), ()))
NN = (((1,), (0,)), ((), ()))


def split(x):
    high = x.astype(BF16)
    low = (x - high.astype(F32)).astype(BF16)
    return high, low


def bdot(a, b, dims):
    return lax.dot_general(a, b, dims, preferred_element_type=F32)


def hdot(a, b, dims=NN):
    return lax.dot_general(a, b, dims, precision=lax.Precision.HIGHEST, preferred_element_type=F32)


def gram_kernel(basis_ref, arrived_ref, out_ref, bb, ab, aa):
    step = pl.program_id(0)

    @pl.when(step == 0)
    def _():
        bb[...] = jnp.zeros_like(bb)
        ab[...] = jnp.zeros_like(ab)
        aa[...] = jnp.zeros_like(aa)

    x = jnp.concatenate(split(basis_ref[...]), axis=0)
    y = jnp.concatenate(split(arrived_ref[...]), axis=0)
    bb[...] += bdot(x, x, NT)
    ab[...] += bdot(y, x, NT)
    aa[...] += bdot(y, y, NT)

    @pl.when(step == pl.num_programs(0) - 1)
    def _():
        nb, ns = basis_ref.shape[0], arrived_ref.shape[0]
        g = bb[...]
        out_ref[0:nb, :] = (g[:nb, :nb] + g[nb:, nb:]) + (g[:nb, nb:] + g[nb:, :nb])
        c = ab[...]
        out_ref[nb : nb + ns, :] = (c[:ns, :nb] + c[ns:, nb:]) + (c[:ns, nb:] + c[ns:, :nb])
        s = aa[...]
        out_ref[nb + ns :, :] = jnp.zeros((out_ref.shape[0] - nb - ns, nb), F32)
        out_ref[nb + ns : nb + 2 * ns, 0:ns] = (s[:ns, :ns] + s[ns:, ns:]) + (s[:ns, ns:] + s[ns:, :ns])


def gram_sums(basis, arrived, chunk):
    nb, rows = basis.shape
    ns = arrived.shape[0]
    height = padded_rows(nb + 2 * ns)
    return pl.pallas_call(
        gram_kernel,
        grid=(rows // chunk,),
        in_specs=[
            pl.BlockSpec((nb, chunk), lambda i: (0, i)),
            pl.BlockSpec((ns, chunk), lambda i: (0, i)),
        ],
        out_specs=pl.BlockSpec((height, nb), lambda i: (0, 0)),
        out_shape=jax.ShapeDtypeStruct((height, nb), F32),
        scratch_shapes=[
            pltpu.VMEM((2 * nb, 2 * nb), F32),
            pltpu.VMEM((2 * ns, 2 * nb), F32),
            pltpu.VMEM((2 * ns, 2 * ns), F32),
        ],
        compiler_params=pltpu.CompilerParams(vmem_limit_bytes=60 << 20),
        name="gram_sums",
    )(basis, arrived)


def exchange_kernel(n_grp, snap_ref, out_ref, ready, held, send_sem, recv_sem):
    me = lax.axis_index("grp")
    row = lax.axis_index("row")
    own = snap_ref.shape[0]
    barrier = pltpu.get_barrier_semaphore()
    for k in range(1, n_grp):
        pl.semaphore_signal(
            barrier, inc=1, device_id=(lax.rem(me + k, n_grp), row), device_id_type=MESH
        )
    for q in range(n_grp):
        ready[q] = snap_ref[:, q, :]
    pl.semaphore_wait(barrier, n_grp - 1)

    def copy(k):
        other = lax.rem(me + k, n_grp)
        return pltpu.make_async_remote_copy(
            src_ref=ready.at[other],
            dst_ref=held.at[k],
            send_sem=send_sem.at[k],
            recv_sem=recv_sem.at[k],
            device_id=(other, row),
            device_id_type=MESH,
        )

    for k in range(1, n_grp):
        copy(k).start()
    held[0] = ready[me]
    for k in range(1, n_grp):
        copy(k).wait()
    for q in range(n_grp):
        out_ref[q * own : (q + 1) * own, :] = held[lax.rem(me - q + n_grp, n_grp)]


def exchange(snapshots):
    own, n_grp, local = snapshots.shape
    return pl.pallas_call(
        functools.partial(exchange_kernel, n_grp),
        in_specs=[pl.BlockSpec(memory_space=pltpu.VMEM)],
        out_specs=pl.BlockSpec(memory_space=pltpu.VMEM),
        out_shape=jax.ShapeDtypeStruct((own * n_grp, local), F32),
        scratch_shapes=[
            pltpu.VMEM((n_grp, own, local), F32),
            pltpu.VMEM((n_grp, own, local), F32),
            pltpu.SemaphoreType.DMA((n_grp,)),
            pltpu.SemaphoreType.DMA((n_grp,)),
        ],
        compiler_params=pltpu.CompilerParams(
            collective_id=3, has_side_effects=True, vmem_limit_bytes=16 << 20
        ),
        name="exchange",
    )(snapshots)


def halo_kernel(n_row, count, new_ref, low_ref, high_ref, send_sem, recv_sem):
    me = lax.axis_index("grp") * n_row + lax.axis_index("row")
    width = low_ref.shape[1]
    local = new_ref.shape[1]
    barrier = pltpu.get_barrier_semaphore()

    def where(device):
        return (device // n_row, lax.rem(device, n_row))

    has_left = me > 0
    has_right = me < count - 1

    for other in (me + 1, me + count - 1):
        pl.semaphore_signal(
            barrier, inc=1, device_id=where(lax.rem(other, count)), device_id_type=MESH
        )
    pl.semaphore_wait(barrier, 2)

    def right():
        return pltpu.make_async_remote_copy(
            src_ref=new_ref.at[:, local - width :],
            dst_ref=low_ref,
            send_sem=send_sem.at[0],
            recv_sem=recv_sem.at[0],
            device_id=where(me + 1),
            device_id_type=MESH,
        )

    def left():
        return pltpu.make_async_remote_copy(
            src_ref=new_ref.at[:, 0:width],
            dst_ref=high_ref,
            send_sem=send_sem.at[1],
            recv_sem=recv_sem.at[1],
            device_id=where(me - 1),
            device_id_type=MESH,
        )

    @pl.when(has_right)
    def _():
        right().start()

    @pl.when(has_left)
    def _():
        left().start()

    @pl.when(jnp.logical_not(has_left))
    def _():
        low_ref[...] = jnp.zeros_like(low_ref)

    @pl.when(jnp.logical_not(has_right))
    def _():
        high_ref[...] = jnp.zeros_like(high_ref)

    @pl.when(has_right)
    def _():
        right().wait_send()
        left().wait_recv()

    @pl.when(has_left)
    def _():
        left().wait_send()
        right().wait_recv()


def halo(new, width):
    n_row = lax.axis_size("row")
    count = lax.axis_size("grp") * n_row
    vmem = pl.BlockSpec(memory_space=pltpu.VMEM)
    side = jax.ShapeDtypeStruct((new.shape[0], width), F32)
    return pl.pallas_call(
        functools.partial(halo_kernel, n_row, count),
        in_specs=[vmem],
        out_specs=[vmem, vmem],
        out_shape=[side, side],
        scratch_shapes=[pltpu.SemaphoreType.DMA((2,)), pltpu.SemaphoreType.DMA((2,))],
        compiler_params=pltpu.CompilerParams(collective_id=4, has_side_effects=True),
        name="halo",
    )(new)


def reduce_kernel(n_grp, n_row, x_ref, out_ref, held, summed, send1, recv1, send2, recv2, send3, recv3):
    mg = lax.axis_index("grp")
    mr = lax.axis_index("row")
    barrier = pltpu.get_barrier_semaphore()

    def greet_row(k, carry):
        pl.semaphore_signal(
            barrier, inc=1, device_id=(mg, lax.rem(mr + k, n_row)), device_id_type=MESH
        )
        return carry

    lax.fori_loop(1, n_row, greet_row, 0)
    for k in range(1, n_grp):
        pl.semaphore_signal(
            barrier, inc=1, device_id=(lax.rem(mg + k, n_grp), mr), device_id_type=MESH
        )
    pl.semaphore_wait(barrier, n_row + n_grp - 2)

    def first(k):
        other = lax.rem(mr + k, n_row)
        return pltpu.make_async_remote_copy(
            src_ref=x_ref.at[other],
            dst_ref=held.at[k],
            send_sem=send1.at[k],
            recv_sem=recv1.at[k],
            device_id=(mg, other),
            device_id_type=MESH,
        )

    def second(k):
        return pltpu.make_async_remote_copy(
            src_ref=summed.at[0],
            dst_ref=summed.at[k],
            send_sem=send2.at[k],
            recv_sem=recv2.at[k],
            device_id=(lax.rem(mg + k, n_grp), mr),
            device_id_type=MESH,
        )

    def third(k, block):
        return pltpu.make_async_remote_copy(
            src_ref=out_ref.at[block],
            dst_ref=out_ref.at[block],
            send_sem=send3.at[k],
            recv_sem=recv3.at[k],
            device_id=(mg, lax.rem(mr + k, n_row)),
            device_id_type=MESH,
        )

    def run(low, high, act):
        def one(k, carry):
            act(k)
            return carry

        lax.fori_loop(low, high, one, 0)

    run(1, n_row, lambda k: first(k).start())
    held[0] = x_ref[mr]
    run(1, n_row, lambda k: first(k).wait_recv())
    summed[0] = jnp.sum(held[...], axis=0)
    run(1, n_grp, lambda k: second(k).start())
    run(1, n_grp, lambda k: second(k).wait())
    total = summed[mg]
    for q in range(1, n_grp):
        total = total + summed[lax.rem(mg + n_grp - q, n_grp)]
    out_ref[mr] = total
    run(1, n_row, lambda k: third(k, mr).start())
    run(1, n_row, lambda k: third(k, lax.rem(mr - k + n_row, n_row)).wait_recv())
    run(1, n_row, lambda k: first(k).wait_send())
    run(1, n_row, lambda k: third(k, mr).wait_send())


def padded_rows(rows):
    step = 8 * lax.axis_size("row")
    return -(-rows // step) * step


def reduce_tiles(x, ident):
    n_row = lax.axis_size("row")
    n_grp = lax.axis_size("grp")
    shape = (n_row, x.shape[0] // n_row, x.shape[1])
    return pl.pallas_call(
        functools.partial(reduce_kernel, n_grp, n_row),
        in_specs=[pl.BlockSpec(memory_space=pltpu.VMEM)],
        out_specs=pl.BlockSpec(memory_space=pltpu.VMEM),
        out_shape=jax.ShapeDtypeStruct(shape, F32),
        scratch_shapes=[
            pltpu.VMEM(shape, F32),
            pltpu.VMEM((n_grp,) + shape[1:], F32),
            pltpu.SemaphoreType.DMA((n_row,)),
            pltpu.SemaphoreType.DMA((n_row,)),
            pltpu.SemaphoreType.DMA((n_grp,)),
            pltpu.SemaphoreType.DMA((n_grp,)),
            pltpu.SemaphoreType.DMA((n_row,)),
            pltpu.SemaphoreType.DMA((n_row,)),
        ],
        compiler_params=pltpu.CompilerParams(collective_id=ident, has_side_effects=True),
        name="reduce_tiles",
    )(x.reshape(shape)).reshape(x.shape)


def factor_kernel(total, sums_ref, assign_ref, basis_ref, arrived_ref, new_ref, coords_ref, r_ref, m, wb, wa):
    nb = basis_ref.shape[0]
    ns = arrived_ref.shape[0]

    @pl.when(pl.program_id(0) == 0)
    def _():
        scale = 1.0 / total
        placing = (
            lax.broadcasted_iota(jnp.int32, (ns, ns), 0) == assign_ref[...]
        ).astype(F32)
        project = hdot(placing, sums_ref[nb : nb + ns, :] * scale)
        snap = hdot(hdot(placing, sums_ref[nb + ns : nb + 2 * ns, 0:ns] * scale), placing, NT)
        m[0:nb, :] = sums_ref[0:nb, :] * scale
        m[nb : nb + ns, :] = project
        lanes = lax.broadcasted_iota(jnp.int32, (1, nb), 1)
        for k in range(nb):
            block = m[...]
            here = lanes == k
            row = block[k : k + 1, :]
            inv = 1.0 / row[:, k : k + 1]
            row = jnp.where(here, inv, row * inv)
            column = block[:, k : k + 1]
            m[...] = jnp.where(here, 0.0, block) - column * row
            m[k : k + 1, :] = row
        coords = -m[nb : nb + ns, :]
        coords_ref[...] = coords
        schur = snap - hdot(project, coords, NT)
        schur = 0.5 * (schur + hdot_transpose(schur))
        rows = lax.broadcasted_iota(jnp.int32, (ns, ns), 0)
        cols = lax.broadcasted_iota(jnp.int32, (ns, ns), 1)
        left = schur
        right = (rows == cols).astype(F32)
        below = lax.broadcasted_iota(jnp.int32, (ns, 1), 0)
        for k in range(ns):
            factor = left[:, k : k + 1] / left[k : k + 1, k : k + 1]
            factor = jnp.where(below > k, factor, 0.0)
            left, right = left - factor * left[k : k + 1, :], right - factor * right[k : k + 1, :]
        diagonal = jnp.sum(jnp.where(rows == cols, left, 0.0), axis=1, keepdims=True)
        root = 1.0 / jnp.sqrt(diagonal)
        r_ref[...] = jnp.where(cols >= rows, left * root, 0.0)
        inverse = right * root
        wb[...] = -hdot(inverse, coords)
        wa[...] = hdot(inverse, placing)

    bw = jnp.concatenate(split(wb[...]), axis=0)
    aw = jnp.concatenate(split(wa[...]), axis=0)
    bh, bl = split(basis_ref[...])
    ah, al = split(arrived_ref[...])
    out = (bdot(bw, bl, NN) + bdot(aw, al, NN)) + (bdot(bw, bh, NN) + bdot(aw, ah, NN))
    new_ref[...] = out[:ns] + out[ns:]


def hdot_transpose(x):
    n = x.shape[0]
    eye = (
        lax.broadcasted_iota(jnp.int32, (n, n), 0) == lax.broadcasted_iota(jnp.int32, (n, n), 1)
    ).astype(F32)
    return hdot(eye, x, NT)


def factor_and_columns(sums, assignment, basis, arrived, total, chunk):
    nb, rows = basis.shape
    ns = arrived.shape[0]
    whole = lambda i: (0, 0)
    return pl.pallas_call(
        functools.partial(factor_kernel, float(total)),
        grid=(rows // chunk,),
        in_specs=[
            pl.BlockSpec(sums.shape, whole),
            pl.BlockSpec((1, ns), whole),
            pl.BlockSpec((nb, chunk), lambda i: (0, i)),
            pl.BlockSpec((ns, chunk), lambda i: (0, i)),
        ],
        out_specs=[
            pl.BlockSpec((ns, chunk), lambda i: (0, i)),
            pl.BlockSpec((ns, nb), whole),
            pl.BlockSpec((ns, ns), whole),
        ],
        out_shape=[
            jax.ShapeDtypeStruct((ns, rows), F32),
            jax.ShapeDtypeStruct((ns, nb), F32),
            jax.ShapeDtypeStruct((ns, ns), F32),
        ],
        scratch_shapes=[
            pltpu.VMEM((nb + ns, nb), F32),
            pltpu.VMEM((ns, nb), F32),
            pltpu.VMEM((ns, ns), F32),
        ],
        compiler_params=pltpu.CompilerParams(vmem_limit_bytes=60 << 20),
        name="factor_and_columns",
    )(sums, assignment.reshape(1, ns), basis, arrived)


def apply_kernel(low_ref, mid_ref, high_ref, visc_ref, off_ref, coef_ref, basis_ref, applied_ref, out_ref, ext, wide, bx, nx, sq):
    step = pl.program_id(0)
    ns, chunk = 16, basis_ref.shape[1]
    nb = basis_ref.shape[0]
    terms, slots = coef_ref.shape[0], coef_ref.shape[1]
    width = low_ref.shape[1] // 128
    count = mid_ref.shape[1] // 128
    per_step = chunk // 256
    halves = ns // 8

    @pl.when(step == 0)
    def _():
        for b in range(width):
            ext[b] = low_ref[:, b * 128 : (b + 1) * 128]
            ext[width + count + b] = high_ref[:, b * 128 : (b + 1) * 128]
        for b in range(count):
            ext[width + b] = mid_ref[:, b * 128 : (b + 1) * 128]
        for ref, start in ((low_ref, 0), (mid_ref, width // 2), (high_ref, (width + count) // 2)):
            for b in range(ref.shape[1] // 256):
                wide[start + b] = jnp.concatenate(split(ref[:, b * 256 : (b + 1) * 256]), axis=0)
        bx[...] = jnp.zeros_like(bx)
        nx[...] = jnp.zeros_like(nx)
        sq[...] = jnp.zeros_like(sq)

    lanes = lax.broadcasted_iota(jnp.int32, (slots, 256), 1)
    depth = lax.broadcasted_iota(jnp.int32, (256, 256), 0)

    def by_lanes(spot, t, first):
        low_index = lax.bitwise_and(spot, 127)
        block_index = lax.shift_right_logical(spot, 7)
        sides = [[] for h in range(halves)]
        for u in range(2):
            part = slice(u * 128, (u + 1) * 128)
            lane = jnp.broadcast_to(low_index[t : t + 1, part], (8, 128))
            block = jnp.broadcast_to(block_index[t : t + 1, part] - u, (8, 128))
            picked = [jnp.zeros((8, 128), F32) for h in range(halves)]
            for b in range(2 * width + 1):
                same = block == b
                for h in range(halves):
                    source = ext[2 * first + u + b, h * 8 : (h + 1) * 8, :]
                    got = jnp.take_along_axis(source, lane, axis=1, mode="promise_in_bounds")
                    picked[h] = jnp.where(same, got, picked[h])
            for h in range(halves):
                sides[h].append(picked[h])
        return [jnp.concatenate(side, axis=1) for side in sides]

    def by_product(spot, t, window):
        low_index = lax.bitwise_and(spot, 255)
        block = jnp.broadcast_to(lax.shift_right_logical(spot, 8)[t : t + 1, :], (8, 256))
        chosen = (depth == low_index[t : t + 1, :]).astype(F32).astype(BF16)
        found = jnp.dot(window, chosen, preferred_element_type=F32)
        picked = [found[g * 8 : (g + 1) * 8, :] for g in range(2 * halves)]
        for b in range(1, width + 1):
            same = block == b
            for g in range(2 * halves):
                at = b * 2 * ns + g * 8
                picked[g] = jnp.where(same, found[at : at + 8, :], picked[g])
        return [picked[h] + picked[halves + h] for h in range(halves)]

    def one(c, carry):
        first = step * per_step + c
        at = pl.ds(pl.multiple_of(c * 256, 256), 256)
        spot = off_ref[:, at] + (lanes + width * 128)
        window = wide[pl.ds(first, width + 1)].reshape((width + 1) * 2 * ns, 256)
        totals = [[jnp.zeros((8, 256), F32) for h in range(halves)] for k in range(terms)]
        for t in range(slots):
            if t < LANE_SLOTS:
                picked = by_lanes(spot, t, first)
            else:
                picked = by_product(spot, t, window)
            for k in range(terms):
                weight = coef_ref[k, t : t + 1, at]
                for h in range(halves):
                    totals[k][h] = totals[k][h] + weight * picked[h]
        for k in range(terms):
            for h in range(halves):
                applied_ref[k, h * 8 : (h + 1) * 8, at] = totals[k][h]
        return carry

    lax.fori_loop(0, per_step, one, 0)

    flat = jnp.concatenate([applied_ref[k] for k in range(terms)], axis=0)
    combined = applied_ref[0]
    across = 0.5 + visc_ref[...].astype(F32) / NPARAM
    same = lax.broadcasted_iota(jnp.int32, (ns, ns), 0) == lax.broadcasted_iota(jnp.int32, (ns, ns), 1)
    viscosity = jnp.sum(jnp.where(same, across, 0.0), axis=1, keepdims=True)
    power = viscosity
    for k in range(1, terms):
        combined = combined + power * applied_ref[k]
        power = power * viscosity
    sq[...] += jnp.sum(combined * combined, axis=1, keepdims=True)
    y = jnp.concatenate(split(flat), axis=0)
    x = jnp.concatenate(split(basis_ref[...]), axis=0)
    here = pl.ds(pl.multiple_of(step * chunk, chunk), chunk)
    z = jnp.concatenate(split(mid_ref[:, here]), axis=0)
    bx[...] += bdot(y, x, NT)
    nx[...] += bdot(y, z, NT)

    @pl.when(step == pl.num_programs(0) - 1)
    def _():
        f = terms * ns
        g = bx[...]
        out_ref[0:f, :] = (g[:f, :nb] + g[f:, nb:]) + (g[:f, nb:] + g[f:, :nb])
        s = nx[...]
        out_ref[f:, :] = jnp.zeros((out_ref.shape[0] - f, nb), F32)
        out_ref[f : 2 * f, 0:ns] = (s[:f, :ns] + s[f:, ns:]) + (s[:f, ns:] + s[f:, :ns])
        out_ref[f : f + ns, ns : ns + 1] = sq[...]


def apply_and_blocks(low, new, high, viscosity, offsets, coefs, basis, chunk):
    nb, rows = basis.shape
    ns = new.shape[0]
    terms, slots = coefs.shape[0], coefs.shape[1]
    width = low.shape[1]
    whole = lambda i: (0, 0)
    blocks = (rows + 2 * width) // 128
    height = padded_rows(2 * terms * ns)
    return pl.pallas_call(
        apply_kernel,
        grid=(rows // chunk,),
        in_specs=[
            pl.BlockSpec((ns, width), whole),
            pl.BlockSpec((ns, rows), whole),
            pl.BlockSpec((ns, width), whole),
            pl.BlockSpec((1, ns), whole),
            pl.BlockSpec((slots, chunk), lambda i: (0, i)),
            pl.BlockSpec((terms, slots, chunk), lambda i: (0, 0, i)),
            pl.BlockSpec((nb, chunk), lambda i: (0, i)),
        ],
        out_specs=[
            pl.BlockSpec((terms, ns, chunk), lambda i: (0, 0, i)),
            pl.BlockSpec((height, nb), whole),
        ],
        out_shape=[
            jax.ShapeDtypeStruct((terms, ns, rows), F32),
            jax.ShapeDtypeStruct((height, nb), F32),
        ],
        scratch_shapes=[
            pltpu.VMEM((blocks, ns, 128), F32),
            pltpu.VMEM((blocks // 2, 2 * ns, 256), BF16),
            pltpu.VMEM((2 * terms * ns, 2 * nb), F32),
            pltpu.VMEM((2 * terms * ns, 2 * ns), F32),
            pltpu.VMEM((ns, 1), F32),
        ],
        compiler_params=pltpu.CompilerParams(vmem_limit_bytes=60 << 20),
        name="apply_and_blocks",
    )(low, new, high, viscosity, offsets, coefs, basis)


def body(snapshots, basis, assignment, param_index, offsets, coefs):
    ns = assignment.shape[0]
    nb, local = basis.shape
    terms = coefs.shape[0]
    devices = lax.axis_size("grp") * lax.axis_size("row")
    total = local * devices
    width = HALO_BLOCKS * 128
    arrived = exchange(snapshots)
    sums = reduce_tiles(gram_sums(basis, arrived, 2048), 1)
    new, coords_t, r_factor = factor_and_columns(sums, assignment, basis, arrived, total, 2048)
    low, high = halo(new, width)
    viscosity = param_index.reshape(1, ns)
    applied, parts = apply_and_blocks(low, new, high, viscosity, offsets, coefs, basis, 1024)
    parts = reduce_tiles(parts, 2) / total
    f = terms * ns
    blocks = jnp.concatenate([parts[:f], parts[f : 2 * f, :ns]], axis=1).reshape(terms, ns, nb + ns)
    return (new, applied, coords_t.T, r_factor, blocks.transpose(0, 2, 1), parts[f : f + ns, ns])


def solution(mesh):
    return jax.shard_map(
        body,
        mesh=mesh,
        in_specs=(
            P("grp", None, "row"),
            P(None, ("grp", "row")),
            P(),
            P(),
            P(None, ("grp", "row")),
            P(None, None, ("grp", "row")),
        ),
        out_specs=(P(None, ("grp", "row")), P(None, None, ("grp", "row")), P(), P(), P(), P()),
        check_vma=False,
    )
```
